32 devices in a mesh: dp: 4 (over y, x), section: 2 (over core), tensor: 4 (over z).
Axes of the slice: x: 2, y: 2, z: 4, core: 2. Of those that a mesh axis runs over, the one named last changes fastest.
Arguments:
- tokens: bfloat16 [512, 16384], P('dp'), may hold values from -9 to 9
- order: int32 [512], replicated, may hold values from 0 to 511, as said below
- segments: int32 [512], replicated, may hold values from 0 to 1, as said below
- gain: float32 [2, 16384], P('section', 'dp'), may hold values from 0.1 to 1.9
- w_query: bfloat16 [2, 16384, 8192], P('section', 'dp', 'tensor'), may hold values from -0.046875 to 0.046875
- key_value_weight: bfloat16 [2, 16384, 8, 256], P('section', 'dp', 'tensor'), may hold values from -0.046875 to 0.046875
- w_out: bfloat16 [2, 8192, 16384], P('section', 'tensor', 'dp'), may hold values from -0.0625 to 0.0625
Outputs:
- layer_out: bfloat16 [512, 16384], P('section', 'dp')
The draws below stay inside these ranges and needn't reach their ends.
Inputs may be any that keep to these rules, and one draw needn't show every extreme that they name: A permutation that moves whole sentences: the rows of one sentence (a run of equal segments within a block of 32 rows) come from consecutive entry rows in order. `segments`: within each block of 32 rows the sentence numbers do not fall and each of 0 to 1 appears.
All inputs are finite; a program needn't handle non-finite values.
Results may differ from the reference program's by a relative error of at most 0.022.
Values may be sent and summed in bfloat16 or wider, within the bound.
A program may use at most 128 MiB of HBM per device.

```python
import math
import jax
import jax.numpy as jnp
from jax import lax

MODEL_WIDTH = 16384
HEAD_WIDTH = 128
KEYVALUE_HEADS = 8
QUERY_HEADS = 64
MICRO_TOKENS = 32
M = 4
SENT = 2
TOKENS = 512
N_DP = 4
N_SECTION = 2
N_TENSOR = 4


def draw_tokens(key, part):
    column = jnp.arange(MODEL_WIDTH, dtype=jnp.float32) / (MODEL_WIDTH - 1)
    scales = 0.35 * jnp.exp(jnp.log(6.0) * column)
    values = jax.random.truncated_normal(jax.random.fold_in(key, 22), -4.0, 4.0, (TOKENS, MODEL_WIDTH), jnp.float32)
    return (values * scales[None, :]).astype(jnp.bfloat16)


def sentence_plan(key):
    block_count = TOKENS // MICRO_TOKENS
    head_lengths = jax.random.randint(jax.random.fold_in(key, 11), (block_count, SENT - 1), 1, MICRO_TOKENS // SENT + 1)
    last_length = MICRO_TOKENS - jnp.sum(head_lengths, axis=1, keepdims=True)
    lengths = jnp.concatenate([head_lengths, last_length], axis=1).astype(jnp.int32)
    bounds = jnp.cumsum(lengths, axis=1)
    position = jnp.arange(MICRO_TOKENS, dtype=jnp.int32)
    sentence_segment_rows = jnp.sum((position[None, :, None] >= bounds[:, None, :SENT - 1]).astype(jnp.int32), axis=2).astype(jnp.int32)
    block_starts = bounds - lengths
    sentence_count = block_count * SENT
    shuffled = jax.random.permutation(jax.random.fold_in(key, 12), sentence_count).astype(jnp.int32)
    flat_lengths = lengths.reshape(-1)
    shuffled_lengths = flat_lengths[shuffled]
    shuffled_starts = (jnp.cumsum(shuffled_lengths) - shuffled_lengths).astype(jnp.int32)
    source_start = jnp.zeros((sentence_count,), jnp.int32).at[shuffled].set(shuffled_starts)
    sentence_ids = jnp.arange(block_count, dtype=jnp.int32)[:, None] * SENT + sentence_segment_rows
    offsets = position[None, :] - jnp.take_along_axis(block_starts, sentence_segment_rows, axis=1)
    order_rows = source_start[sentence_ids] + offsets
    return (order_rows.reshape(-1).astype(jnp.int32), sentence_segment_rows.reshape(-1).astype(jnp.int32))


def draw_order(key, part):
    return sentence_plan(key)[0]


def draw_segments(key, part):
    return sentence_plan(key)[1]


def steps_of(key, dims, cuts, smallest, top_value):
    def one(dim, parts):
        heights = jax.random.uniform(jax.random.fold_in(jax.random.fold_in(key, 6), dim), (parts,), jnp.float32, smallest / len(cuts), top_value / len(cuts))
        return jnp.repeat(jnp.exp(heights), dims[dim] // parts).reshape((-1,) + (1,) * (len(dims) - dim - 1))

    loudness = one(*cuts[0])
    for cut in cuts[1:]:
        loudness = loudness * one(*cut)
    return loudness


def gaussian(rng, shape, deviation, most, shards=(), kind=jnp.bfloat16):
    drawn = jax.random.normal(rng, shape, jnp.float32) * deviation
    if len(shards) > 0:
        drawn = steps_of(rng, shape, shards, -0.22, 0.18) * drawn
    return jnp.clip(drawn, min=-most, max=most).astype(kind)


def setup_inputs(seed: int = 0) -> dict:
    key_of = jax.random.split(jax.random.key(seed), 8)
    tokens = draw_tokens(jax.random.fold_in(key_of[7], 71), 0)
    order = draw_order(jax.random.fold_in(key_of[7], 71), 0)
    segments = draw_segments(jax.random.fold_in(key_of[7], 71), 0)
    gain = jnp.clip(1.0 + 0.18 * jax.random.normal(key_of[3], (N_SECTION, MODEL_WIDTH), jnp.float32), 0.1, 1.9)
    w_query = gaussian(key_of[4], (N_SECTION, MODEL_WIDTH, QUERY_HEADS * HEAD_WIDTH), MODEL_WIDTH ** -0.5, 0.046875, ((0, 2), (1, 4), (2, 4)))
    key_value_weight = gaussian(key_of[5], (N_SECTION, MODEL_WIDTH, KEYVALUE_HEADS, 2 * HEAD_WIDTH), MODEL_WIDTH ** -0.5, 0.046875, ((0, 2), (1, 4), (2, 4)))
    w_out = gaussian(key_of[6], (N_SECTION, QUERY_HEADS * HEAD_WIDTH, MODEL_WIDTH), (QUERY_HEADS * HEAD_WIDTH) ** -0.5, 0.0625, ((0, 2), (1, 4), (2, 4)))
    return {"tokens": tokens, "order": order, "segments": segments, "gain": gain, "w_query": w_query, "key_value_weight": key_value_weight, "w_out": w_out}


norm_epsilon = 1e-05

def attention_blocks(query_rows, key_value_rows, sentence_segment_rows):
    query_group_width = QUERY_HEADS // KEYVALUE_HEADS
    query_head_rows = query_rows.astype(jnp.float32).reshape(N_DP, MICRO_TOKENS, KEYVALUE_HEADS, query_group_width, HEAD_WIDTH)
    query_key_pairs = key_value_rows.astype(jnp.float32).reshape(N_DP, MICRO_TOKENS, KEYVALUE_HEADS, 2 * HEAD_WIDTH)
    key_heads = query_key_pairs[..., :HEAD_WIDTH]
    value_heads = query_key_pairs[..., HEAD_WIDTH:]
    scores = jnp.einsum('bqkgd,bskd->bkgqs', query_head_rows, key_heads) / math.sqrt(HEAD_WIDTH)
    position = jnp.arange(MICRO_TOKENS)
    causal = position[None, :] <= position[:, None]
    allowed = (sentence_segment_rows[:, :, None] == sentence_segment_rows[:, None, :]) & causal[None]
    raw_weights = jnp.where(allowed[:, None, None], jnp.exp(scores), 0.0)
    totals = lax.optimization_barrier(jnp.sum(raw_weights, axis=-1, keepdims=True))
    probs = (raw_weights / totals).astype(jnp.bfloat16)
    attended_rows = jnp.einsum('bkgqs,bskd->bqkgd', probs.astype(jnp.float32), value_heads)
    return attended_rows.astype(jnp.bfloat16).reshape(N_DP * MICRO_TOKENS, QUERY_HEADS * HEAD_WIDTH)

def section_layer(hidden, sentence_segment_rows, gain_row, query_weight, key_value_matrix, out_weight):
    widened = hidden.astype(jnp.float32)
    root_mean_square = jnp.sqrt(lax.optimization_barrier(jnp.sum(widened * widened, axis=1)) / MODEL_WIDTH + norm_epsilon)
    normed_rows = (widened * gain_row[None, :]).astype(jnp.bfloat16)
    query_rows = (jnp.dot(normed_rows, query_weight, preferred_element_type=jnp.float32) / root_mean_square[:, None]).astype(jnp.bfloat16)
    key_value_rows = (jnp.dot(normed_rows, key_value_matrix.reshape(MODEL_WIDTH, KEYVALUE_HEADS * 2 * HEAD_WIDTH), preferred_element_type=jnp.float32) / root_mean_square[:, None]).astype(jnp.bfloat16)
    attended_rows = attention_blocks(query_rows, key_value_rows, sentence_segment_rows)
    block_width = QUERY_HEADS * HEAD_WIDTH // N_TENSOR
    total = jnp.zeros(widened.shape, jnp.float32)
    for tensor_rank in range(N_TENSOR):
        lower = tensor_rank * block_width
        upper = lower + block_width
        partial_term = jnp.dot(attended_rows[:, lower:upper], out_weight[lower:upper], preferred_element_type=jnp.float32)
        rounded = lax.optimization_barrier(partial_term.astype(jnp.bfloat16))
        total = total + rounded.astype(jnp.float32)
    return (widened + total).astype(jnp.bfloat16)

def reference(tokens, order, segments, gain, w_query, key_value_weight, w_out):
    arranged = jnp.take(tokens, order, axis=0)
    rows_all = N_DP * MICRO_TOKENS
    finished = []
    for micro_index in range(M):
        hidden = arranged[micro_index * rows_all:(micro_index + 1) * rows_all]
        sentence_segment_rows = segments[micro_index * rows_all:(micro_index + 1) * rows_all].reshape(N_DP, MICRO_TOKENS)
        for layer_index in range(N_SECTION):
            hidden = section_layer(hidden, sentence_segment_rows, gain[layer_index], w_query[layer_index], key_value_weight[layer_index], w_out[layer_index])
        finished.append(hidden)
    return jnp.concatenate(finished, axis=0)
```

```python
import functools
import math

import jax
import jax.numpy as jnp
from jax import lax
from jax.experimental import pallas as pl
from jax.experimental.pallas import tpu as pltpu
from jax.sharding import PartitionSpec as P

KEYVALUE_HEADS = 8
QUERY_HEADS = 64
HEAD = 128
BLOCK = 32
M = 4
QCHUNKS = 5
CHUNKS = 8
LAG = 2

norm_epsilon = 1e-05
MESH = pl.DeviceIdType.MESH


def kernel(
    D, T,
    tokens, order_col, seg_col, seg_row, gain, wq, wkv, wo,
    out,
    wqkv_v, wo_v, ent, xb, sc, qp, qr, sqp, sqr, mix, zs, zr,
    w_sem, wo_sem, own_sem, a_s, a_r, q_s, q_r, n_s, n_r, m_s, m_r,
    z_s, z_r, t_s, h_s, h_r, l_s,
):
    d = lax.axis_index("dp")
    s = lax.axis_index("section")
    t = lax.axis_index("tensor")
    R = D * BLOCK
    W = xb.shape[1]
    rows_in = tokens.shape[0]
    wc = W // CHUNKS
    qw = qp.shape[1]
    qc = qw // QCHUNKS
    half = T // 2
    is_left = t < half
    inward = jnp.where(is_left, t + 1, t - 1)
    outward = jnp.where(is_left, t - 1, t + 1)
    outer = jnp.logical_or(t == 0, t == T - 1)
    middle = jnp.logical_or(t == half - 1, t == half)
    kind = jnp.where(middle, 1, 0)
    kv_heads = KEYVALUE_HEADS // T
    group = QUERY_HEADS // KEYVALUE_HEADS
    qcols = kv_heads * group * HEAD
    peers = [lax.rem(d + r, D) for r in range(1, D)]

    def remote(src, dst, ss, rs, **where):
        return pltpu.make_async_remote_copy(
            src_ref=src, dst_ref=dst, send_sem=ss, recv_sem=rs,
            device_id=where, device_id_type=MESH,
        )

    def cols(c, width):
        return pl.ds(pl.multiple_of(c * width, width), width)

    def rows(start, count):
        return pl.ds(pl.multiple_of(start, BLOCK), count)

    def w_copy(j):
        if j < QCHUNKS - 1:
            return pltpu.make_async_copy(
                wq.at[:, pl.ds(j * qc, qc)], wqkv_v.at[:, pl.ds(j * qc, qc)], w_sem.at[j]
            )
        return pltpu.make_async_copy(wkv, wqkv_v.at[:, pl.ds(j * qc, qc)], w_sem.at[j])

    def wo_copy(c):
        return pltpu.make_async_copy(
            wo.at[:, cols(c, wc)], wo_v.at[:, cols(c, wc)], wo_sem.at[c]
        )

    own_tokens = pltpu.make_async_copy(
        tokens.at[:, cols(d, W)], ent.at[rows(d * rows_in, rows_in)], own_sem
    )

    def entry(r):
        peer = peers[r]
        return remote(
            tokens.at[:, cols(peer, W)], ent.at[rows(d * rows_in, rows_in)],
            a_s.at[r], a_r.at[r], dp=peer,
        )

    barrier = pltpu.get_barrier_semaphore()
    for peer in peers:
        pl.semaphore_signal(barrier, inc=1, device_id={"dp": peer}, device_id_type=MESH)
    pl.semaphore_signal(barrier, inc=1, device_id={"section": 1 - s}, device_id_type=MESH)

    @pl.when(t > 0)
    def _():
        pl.semaphore_signal(barrier, inc=1, device_id={"tensor": t - 1}, device_id_type=MESH)

    @pl.when(t < T - 1)
    def _():
        pl.semaphore_signal(barrier, inc=1, device_id={"tensor": t + 1}, device_id_type=MESH)

    pl.semaphore_wait(barrier, D + jnp.where(t > 0, 1, 0) + jnp.where(t < T - 1, 1, 0))

    @pl.when(s == 0)
    def _():
        for r in range(D - 1):
            entry(r).start()
        own_tokens.start()

    for j in range(QCHUNKS):
        w_copy(j).start()
    for c in range(CHUNKS):
        wo_copy(c).start()

    @pl.when(s == 0)
    def _():
        own_tokens.wait()
        for r in range(D - 1):
            entry(r).wait_recv()

    def micro(m, carry):
        slot = lax.rem(m, 2)
        mrow = m * R

        def handed(c):
            return remote(
                xb.at[:, cols(c, wc)], ent.at[rows(mrow, R), cols(c, wc)],
                h_s.at[c], h_r.at[m, c], section=1 - s,
            )

        def finished_away(c):
            return remote(
                xb.at[:, cols(c, wc)], out.at[rows(mrow, R), cols(c, wc)],
                h_s.at[c], h_r.at[m, c], section=1 - s,
            )

        def finished_here(c):
            return pltpu.make_async_copy(
                xb.at[:, cols(c, wc)],
                out.at[rows((m - M // 2) * R, R), cols(c, wc)],
                l_s.at[c],
            )

        @pl.when(s == 0)
        def _():
            width = M * R
            pick = (
                order_col[rows(mrow, R), :]
                == lax.broadcasted_iota(jnp.int32, (R, width), 1)
            ).astype(jnp.float32).astype(jnp.bfloat16)

            def take(c, _):
                xb[:, cols(c, wc)] = jnp.dot(
                    pick, ent[:, cols(c, wc)], preferred_element_type=jnp.float32
                ).astype(jnp.bfloat16)
                return 0

            lax.fori_loop(0, CHUNKS, take, 0)

        @pl.when(s == 1)
        def _():
            def take(c, _):
                handed(c).wait_recv()
                xb[:, cols(c, wc)] = ent[rows(mrow, R), cols(c, wc)]
                return 0

            lax.fori_loop(0, CHUNKS, take, 0)

        def scale(c, total):
            wide = xb[:, cols(c, wc)].astype(jnp.float32)
            sc[:, cols(c, wc)] = (wide * gain[:, cols(c, wc)]).astype(jnp.bfloat16)
            square = wide * wide
            for k in range(wc // 128):
                total = total + square[:, k * 128 : (k + 1) * 128]
            return total

        squares = lax.fori_loop(0, CHUNKS, scale, jnp.zeros((R, 128), jnp.float32))
        sqp[...] = squares

        def norm_copy(r):
            return remote(
                sqp.at[rows(peers[r] * BLOCK, BLOCK)], sqr.at[slot, r],
                n_s.at[r], n_r.at[slot, r], dp=peers[r],
            )

        def q_copy(r, j):
            return remote(
                qp.at[rows(peers[r] * BLOCK, BLOCK), cols(j, qc)],
                qr.at[slot, r, :, cols(j, qc)],
                q_s.at[r, j], q_r.at[slot, r, j], dp=peers[r],
            )

        for r in range(D - 1):
            norm_copy(r).start()

        @pl.when(m == 0)
        def _():
            for j in range(QCHUNKS):
                w_copy(j).wait()

        def project(j, _):
            qp[:, cols(j, qc)] = jnp.dot(
                sc[...], wqkv_v[:, cols(j, qc)], preferred_element_type=jnp.float32
            ).astype(jnp.bfloat16)
            for r in range(D - 1):
                q_copy(r, j).start()
            return 0

        lax.fori_loop(0, QCHUNKS, project, 0)

        own = rows(d * BLOCK, BLOCK)
        for r in range(D - 1):
            norm_copy(r).wait_recv()
        square = sqp[own, :]
        for r in range(D - 1):
            square = square + sqr[slot, r]
        rms = jnp.sqrt(
            jnp.sum(square, axis=1, keepdims=True) / (W * D) + norm_epsilon
        )

        def arrived(j, _):
            for r in range(D - 1):
                q_copy(r, j).wait_recv()
            return 0

        lax.fori_loop(0, QCHUNKS, arrived, 0)

        def summed(start, width):
            total = qp[own, pl.ds(start, width)].astype(jnp.float32)
            for r in range(D - 1):
                total = total + qr[slot, r, :, pl.ds(start, width)].astype(jnp.float32)
            return (total / rms).astype(jnp.bfloat16)

        base = mrow + d * BLOCK
        same = seg_col[rows(base, BLOCK), :] == seg_row[pl.ds(m * D + d, 1), :]
        later = lax.broadcasted_iota(jnp.int32, (BLOCK, BLOCK), 1)
        here = lax.broadcasted_iota(jnp.int32, (BLOCK, BLOCK), 0)
        allowed = jnp.where(jnp.logical_and(same, later <= here), 1, 0)
        allowed = jnp.concatenate([allowed] * group, axis=0) != 0

        def mix_copy(r, h):
            part = mix.at[slot, own, pl.ds(h * group * HEAD, group * HEAD)]
            return remote(
                part, part, m_s.at[r, h], m_r.at[slot, r, h], dp=peers[r]
            )

        for h in range(kv_heads):
            lower = h * group * HEAD
            query = jnp.concatenate(
                [summed(lower + g * HEAD, HEAD) for g in range(group)], axis=0
            )
            key = summed(qcols + h * 2 * HEAD, HEAD)
            value = summed(qcols + h * 2 * HEAD + HEAD, HEAD)
            scores = lax.dot_general(
                query, key, (((1,), (1,)), ((), ())), preferred_element_type=jnp.float32
            ) / math.sqrt(HEAD)
            weights = jnp.where(allowed, jnp.exp(scores), 0.0)
            probs = (weights / jnp.sum(weights, axis=1, keepdims=True)).astype(jnp.bfloat16)
            mixed = jnp.dot(probs, value, preferred_element_type=jnp.float32).astype(
                jnp.bfloat16
            )
            for g in range(group):
                mix[slot, own, pl.ds(lower + g * HEAD, HEAD)] = mixed[
                    g * BLOCK : (g + 1) * BLOCK
                ]
            for r in range(D - 1):
                mix_copy(r, h).start()

        @pl.when(m == 0)
        def _():
            for c in range(CHUNKS):
                wo_copy(c).wait()

        for h in range(kv_heads):
            for r in range(D - 1):
                mix_copy(r, h).wait_recv()

        def inward_copy(c):
            return remote(
                zs.at[:, cols(c, wc)], zr.at[kind, slot, :, cols(c, wc)],
                z_s.at[c], z_r.at[kind, slot, c], tensor=inward,
            )

        def from_outside(c):
            return remote(
                zs.at[:, cols(c, wc)], zr.at[0, slot, :, cols(c, wc)],
                z_s.at[c], z_r.at[0, slot, c], tensor=inward,
            )

        def outward_copy(c):
            return remote(
                xb.at[:, cols(c, wc)], zr.at[1, slot, :, cols(c, wc)],
                t_s.at[c], z_r.at[1, slot, c], tensor=outward,
            )

        def partial(c, _):
            zs[:, cols(c, wc)] = jnp.dot(
                mix[slot], wo_v[:, cols(c, wc)], preferred_element_type=jnp.float32
            ).astype(jnp.bfloat16)

            @pl.when(outer)
            def _():
                inward_copy(c).start()

            return 0

        lax.fori_loop(0, CHUNKS, partial, 0)

        def relay(step, _):
            @pl.when(jnp.logical_and(jnp.logical_not(outer), step < CHUNKS))
            def _():
                from_outside(step).wait_recv()
                zs[:, cols(step, wc)] = (
                    zs[:, cols(step, wc)].astype(jnp.float32)
                    + zr[0, slot, :, cols(step, wc)].astype(jnp.float32)
                ).astype(jnp.bfloat16)
                inward_copy(step).start()

            @pl.when(step >= LAG)
            def _():
                c = step - LAG
                outward_copy(c).wait_recv()

                @pl.when(middle)
                def _():
                    xb[:, cols(c, wc)] = (
                        xb[:, cols(c, wc)].astype(jnp.float32)
                        + (
                            zs[:, cols(c, wc)].astype(jnp.float32)
                            + zr[1, slot, :, cols(c, wc)].astype(jnp.float32)
                        )
                    ).astype(jnp.bfloat16)

                @pl.when(jnp.logical_not(middle))
                def _():
                    xb[:, cols(c, wc)] = zr[1, slot, :, cols(c, wc)]

                @pl.when(jnp.logical_not(outer))
                def _():
                    outward_copy(c).start()

                @pl.when(s == 0)
                def _():
                    handed(c).start()

                @pl.when(jnp.logical_and(s == 1, m < M // 2))
                def _():
                    finished_away(c).start()

                @pl.when(jnp.logical_and(s == 1, m >= M // 2))
                def _():
                    finished_here(c).start()

            return 0

        lax.fori_loop(0, CHUNKS + LAG, relay, 0)

        def sent(c, _):
            inward_copy(c).wait_send()

            @pl.when(jnp.logical_not(outer))
            def _():
                outward_copy(c).wait_send()

            @pl.when(s == 0)
            def _():
                handed(c).wait_send()

            @pl.when(jnp.logical_and(s == 1, m < M // 2))
            def _():
                finished_away(c).wait_send()

            @pl.when(jnp.logical_and(s == 1, m >= M // 2))
            def _():
                finished_here(c).wait()

            return 0

        lax.fori_loop(0, CHUNKS, sent, 0)

        def q_sent(j, _):
            for r in range(D - 1):
                q_copy(r, j).wait_send()
            return 0

        lax.fori_loop(0, QCHUNKS, q_sent, 0)
        for r in range(D - 1):
            norm_copy(r).wait_send()
            for h in range(kv_heads):
                mix_copy(r, h).wait_send()
        return carry

    lax.fori_loop(0, M, micro, 0)

    @pl.when(s == 0)
    def _():
        for r in range(D - 1):
            entry(r).wait_send()

        def returned(i, _):
            m, c = i // CHUNKS, lax.rem(i, CHUNKS)
            remote(
                xb.at[:, cols(c, wc)], out.at[rows(m * R, R), cols(c, wc)],
                h_s.at[c], h_r.at[m, c], section=1 - s,
            ).wait_recv()
            return 0

        lax.fori_loop(0, (M // 2) * CHUNKS, returned, 0)


def on_device(D, T, tokens, order, segments, gain, w_query, key_value_weight, w_out):
    R = D * BLOCK
    W = gain.shape[1]
    qcols = w_query.shape[2]
    wkv = key_value_weight[0].reshape(W, -1)
    qw = qcols + wkv.shape[1]
    kv_heads = key_value_weight.shape[2]
    bf16, f32 = jnp.bfloat16, jnp.float32
    vmem, hbm = pl.BlockSpec(memory_space=pltpu.VMEM), pl.BlockSpec(memory_space=pl.ANY)
    dma = pltpu.SemaphoreType.DMA
    return pl.pallas_call(
        functools.partial(kernel, D, T),
        out_shape=jax.ShapeDtypeStruct((M // 2 * R, W), bf16),
        in_specs=[hbm, vmem, vmem, vmem, vmem, hbm, hbm, hbm],
        out_specs=hbm,
        scratch_shapes=[
            pltpu.VMEM((W, qw), bf16),
            pltpu.VMEM((qcols, W), bf16),
            pltpu.VMEM((M * R, W), bf16),
            pltpu.VMEM((R, W), bf16),
            pltpu.VMEM((R, W), bf16),
            pltpu.VMEM((R, qw), bf16),
            pltpu.VMEM((2, D - 1, BLOCK, qw), bf16),
            pltpu.VMEM((R, 128), f32),
            pltpu.VMEM((2, D - 1, BLOCK, 128), f32),
            pltpu.VMEM((2, R, qcols), bf16),
            pltpu.VMEM((R, W), bf16),
            pltpu.VMEM((2, 2, R, W), bf16),
            dma((QCHUNKS,)),
            dma((CHUNKS,)),
            dma,
            dma((D - 1,)),
            dma((D - 1,)),
            dma((D - 1, QCHUNKS)),
            dma((2, D - 1, QCHUNKS)),
            dma((D - 1,)),
            dma((2, D - 1)),
            dma((D - 1, kv_heads)),
            dma((2, D - 1, kv_heads)),
            dma((CHUNKS,)),
            dma((2, 2, CHUNKS)),
            dma((CHUNKS,)),
            dma((CHUNKS,)),
            dma((M, CHUNKS)),
            dma((CHUNKS,)),
        ],
        compiler_params=pltpu.CompilerParams(
            collective_id=0, has_side_effects=True, vmem_limit_bytes=62 * 1024 * 1024
        ),
    )(
        tokens,
        order[:, None],
        segments[:, None],
        segments.reshape(M * D, BLOCK),
        gain,
        w_query[0],
        wkv,
        w_out[0],
    )


def solution(mesh):
    placed = (
        P("dp", None),
        P(),
        P(),
        P("section", "dp"),
        P("section", "dp", "tensor"),
        P("section", "dp", "tensor", None),
        P("section", "tensor", "dp"),
    )
    return jax.shard_map(
        functools.partial(on_device, mesh.shape["dp"], mesh.shape["tensor"]),
        mesh=mesh, in_specs=placed, out_specs=P("section", "dp"), check_vma=False,
    )
```

```python
import functools
import math

import jax
import jax.numpy as jnp
from jax import lax
from jax.experimental import pallas as pl
from jax.experimental.pallas import tpu as pltpu
from jax.sharding import PartitionSpec as P

KEYVALUE_HEADS = 8
QUERY_HEADS = 64
HEAD = 128
BLOCK = 32
M = 4
QCHUNKS = 5
CHUNKS = 8
EARLY = 3
LAG = 2

norm_epsilon = 1e-05
MESH = pl.DeviceIdType.MESH


def kernel(
    D, T,
    tokens, order, segments, gain, wq, wkv, wo,
    out,
    wqkv_v, wo_v, ent, pick, xb, sc, qp, qr, sqp, sqr, mix, zs, zr,
    w_sem, wo_sem, own_sem, a_s, a_r, q_s, q_r, n_s, n_r, m_s, m_r,
    z_s, z_r, t_s, h_s, h_r, l_s,
):
    d = lax.axis_index("dp")
    s = lax.axis_index("section")
    t = lax.axis_index("tensor")
    R = D * BLOCK
    W = xb.shape[2]
    rows_in = tokens.shape[0]
    wc = W // CHUNKS
    qw = qp.shape[1]
    qc = qw // QCHUNKS
    half = T // 2
    is_left = t < half
    inward = jnp.where(is_left, t + 1, t - 1)
    outward = jnp.where(is_left, t - 1, t + 1)
    outer = jnp.logical_or(t == 0, t == T - 1)
    middle = jnp.logical_or(t == half - 1, t == half)
    kind = jnp.where(middle, 1, 0)
    kv_heads = KEYVALUE_HEADS // T
    group = QUERY_HEADS // KEYVALUE_HEADS
    qcols = kv_heads * group * HEAD
    peers = [lax.rem(d + r, D) for r in range(1, D)]

    def remote(src, dst, ss, rs, **where):
        return pltpu.make_async_remote_copy(
            src_ref=src, dst_ref=dst, send_sem=ss, recv_sem=rs,
            device_id=where, device_id_type=MESH,
        )

    def cols(c, width):
        return pl.ds(pl.multiple_of(c * width, width), width)

    def rows(start, count):
        return pl.ds(pl.multiple_of(start, BLOCK), count)

    def w_copy(j):
        if j < QCHUNKS - 1:
            return pltpu.make_async_copy(
                wq.at[:, pl.ds(j * qc, qc)], wqkv_v.at[:, pl.ds(j * qc, qc)], w_sem.at[j]
            )
        return pltpu.make_async_copy(wkv, wqkv_v.at[:, pl.ds(j * qc, qc)], w_sem.at[j])

    def wo_copy(c):
        return pltpu.make_async_copy(
            wo.at[:, cols(c, wc)], wo_v.at[:, cols(c, wc)], wo_sem.at[c]
        )

    own_tokens = pltpu.make_async_copy(
        tokens.at[:, cols(d, W)], ent.at[rows(d * rows_in, rows_in)], own_sem
    )

    def entry(r):
        peer = peers[r]
        return remote(
            tokens.at[:, cols(peer, W)], ent.at[rows(d * rows_in, rows_in)],
            a_s.at[r], a_r.at[r], dp=peer,
        )

    barrier = pltpu.get_barrier_semaphore()
    for peer in peers:
        pl.semaphore_signal(barrier, inc=1, device_id={"dp": peer}, device_id_type=MESH)
    pl.semaphore_signal(barrier, inc=1, device_id={"section": 1 - s}, device_id_type=MESH)

    @pl.when(t > 0)
    def _():
        pl.semaphore_signal(barrier, inc=1, device_id={"tensor": t - 1}, device_id_type=MESH)

    @pl.when(t < T - 1)
    def _():
        pl.semaphore_signal(barrier, inc=1, device_id={"tensor": t + 1}, device_id_type=MESH)

    pl.semaphore_wait(barrier, D + jnp.where(t > 0, 1, 0) + jnp.where(t < T - 1, 1, 0))

    @pl.when(s == 0)
    def _():
        for r in range(D - 1):
            entry(r).start()
        own_tokens.start()

    for j in range(QCHUNKS):
        w_copy(j).start()
    for c in range(CHUNKS):
        wo_copy(c).start()

    @pl.when(s == 0)
    def _():
        own_tokens.wait()
        for r in range(D - 1):
            entry(r).wait_recv()

    def handed(n, c):
        return remote(
            xb.at[lax.rem(n, 2), :, cols(c, wc)], ent.at[rows(n * R, R), cols(c, wc)],
            h_s.at[c], h_r.at[n, c], section=1 - s,
        )

    def norm_copy(n, r):
        return remote(
            sqp.at[rows(peers[r] * BLOCK, BLOCK)], sqr.at[lax.rem(n, 2), r],
            n_s.at[r], n_r.at[lax.rem(n, 2), r], dp=peers[r],
        )

    def q_copy(n, r, j):
        return remote(
            qp.at[rows(peers[r] * BLOCK, BLOCK), cols(j, qc)],
            qr.at[lax.rem(n, 2), r, :, cols(j, qc)],
            q_s.at[r, j], q_r.at[lax.rem(n, 2), r, j], dp=peers[r],
        )

    def choose(n):
        line = order[pl.ds(pl.multiple_of(n * R, R), R)].astype(jnp.float32)[None, :]
        down = lax.broadcasted_iota(jnp.int32, (R, R), 0)
        across = lax.broadcasted_iota(jnp.int32, (R, R), 1)
        column = jnp.sum(jnp.where(down == across, line, 0.0), axis=1, keepdims=True)
        places = lax.broadcasted_iota(jnp.int32, (R, M * R), 1).astype(jnp.float32)
        pick[...] = jnp.where(column == places, 1.0, 0.0).astype(jnp.bfloat16)

    def take(n, c):
        xb[lax.rem(n, 2), :, cols(c, wc)] = jnp.dot(
            pick[...], ent[:, cols(c, wc)], preferred_element_type=jnp.float32
        ).astype(jnp.bfloat16)

    def scale(n):
        @pl.when(s == 1)
        def _():
            def received(c, _):
                handed(n, c).wait_recv()
                xb[lax.rem(n, 2), :, cols(c, wc)] = ent[rows(n * R, R), cols(c, wc)]
                return 0

            lax.fori_loop(0, CHUNKS, received, 0)

        def one(c, total):
            wide = xb[lax.rem(n, 2), :, cols(c, wc)].astype(jnp.float32)
            sc[:, cols(c, wc)] = (wide * gain[:, cols(c, wc)]).astype(jnp.bfloat16)
            square = wide * wide
            for k in range(wc // 128):
                total = total + square[:, k * 128 : (k + 1) * 128]
            return total

        sqp[...] = lax.fori_loop(0, CHUNKS, one, jnp.zeros((R, 128), jnp.float32))
        for r in range(D - 1):
            norm_copy(n, r).start()

    def project(n, j):
        qp[:, cols(j, qc)] = jnp.dot(
            sc[...], wqkv_v[:, cols(j, qc)], preferred_element_type=jnp.float32
        ).astype(jnp.bfloat16)
        for r in range(D - 1):
            q_copy(n, r, j).start()

    @pl.when(s == 0)
    def _():
        choose(0)

        def first_take(c, _):
            take(0, c)
            return 0

        lax.fori_loop(0, CHUNKS, first_take, 0)

    scale(0)
    for j in range(QCHUNKS):
        w_copy(j).wait()

    def first_project(j, _):
        project(0, j)
        return 0

    lax.fori_loop(0, QCHUNKS, first_project, 0)

    own = rows(d * BLOCK, BLOCK)

    def micro(m, carry):
        slot = lax.rem(m, 2)
        mrow = m * R
        xm = xb.at[slot]

        def finished_away(c):
            return remote(
                xm.at[:, cols(c, wc)], out.at[rows(mrow, R), cols(c, wc)],
                h_s.at[c], h_r.at[m, c], section=1 - s,
            )

        def finished_here(c):
            return pltpu.make_async_copy(
                xm.at[:, cols(c, wc)],
                out.at[rows((m - M // 2) * R, R), cols(c, wc)],
                l_s.at[c],
            )

        line = segments[pl.ds(pl.multiple_of(mrow, R), R)].astype(jnp.float32)[None, :]
        down = lax.broadcasted_iota(jnp.int32, (BLOCK, R), 0) + d * BLOCK
        mine = down == lax.broadcasted_iota(jnp.int32, (BLOCK, R), 1)
        column = jnp.sum(jnp.where(mine, line, 0.0), axis=1, keepdims=True)
        same = jnp.where(column == line, 1.0, 0.0).astype(jnp.bfloat16)
        same = lax.dot_general(
            same, jnp.where(mine, 1.0, 0.0).astype(jnp.bfloat16),
            (((1,), (1,)), ((), ())), preferred_element_type=jnp.float32,
        )
        causal = lax.broadcasted_iota(jnp.int32, (BLOCK, BLOCK), 1) <= (
            lax.broadcasted_iota(jnp.int32, (BLOCK, BLOCK), 0)
        )
        allowed = jnp.where(causal, same, 0.0)
        allowed = jnp.concatenate([allowed] * group, axis=0) > 0.5

        for r in range(D - 1):
            norm_copy(m, r).wait_recv()
        square = sqp[own, :]
        for r in range(D - 1):
            square = square + sqr[slot, r]
        rms = jnp.sqrt(
            jnp.sum(square, axis=1, keepdims=True) / (W * D) + norm_epsilon
        )

        def arrived(j, _):
            for r in range(D - 1):
                q_copy(m, r, j).wait_recv()
            return 0

        lax.fori_loop(0, QCHUNKS, arrived, 0)

        def summed(start, width):
            total = qp[own, pl.ds(start, width)].astype(jnp.float32)
            for r in range(D - 1):
                total = total + qr[slot, r, :, pl.ds(start, width)].astype(jnp.float32)
            return (total / rms).astype(jnp.bfloat16)

        def mix_copy(r, h):
            part = mix.at[slot, own, pl.ds(h * group * HEAD, group * HEAD)]
            return remote(
                part, part, m_s.at[r, h], m_r.at[slot, r, h], dp=peers[r]
            )

        for h in range(kv_heads):
            lower = h * group * HEAD
            query = jnp.concatenate(
                [summed(lower + g * HEAD, HEAD) for g in range(group)], axis=0
            )
            key = summed(qcols + h * 2 * HEAD, HEAD)
            value = summed(qcols + h * 2 * HEAD + HEAD, HEAD)
            scores = lax.dot_general(
                query, key, (((1,), (1,)), ((), ())), preferred_element_type=jnp.float32
            ) / math.sqrt(HEAD)
            weights = jnp.where(allowed, jnp.exp(scores), 0.0)
            probs = (weights / jnp.sum(weights, axis=1, keepdims=True)).astype(jnp.bfloat16)
            mixed = jnp.dot(probs, value, preferred_element_type=jnp.float32).astype(
                jnp.bfloat16
            )
            for g in range(group):
                mix[slot, own, pl.ds(lower + g * HEAD, HEAD)] = mixed[
                    g * BLOCK : (g + 1) * BLOCK
                ]
            for r in range(D - 1):
                mix_copy(r, h).start()

        def q_sent(j, _):
            for r in range(D - 1):
                q_copy(m, r, j).wait_send()
            return 0

        lax.fori_loop(0, QCHUNKS, q_sent, 0)
        for r in range(D - 1):
            norm_copy(m, r).wait_send()

        @pl.when(jnp.logical_and(s == 0, m + 1 < M))
        def _():
            choose(m + 1)

        @pl.when(m == 0)
        def _():
            for c in range(CHUNKS):
                wo_copy(c).wait()

        for h in range(kv_heads):
            for r in range(D - 1):
                mix_copy(r, h).wait_recv()

        def inward_copy(c):
            return remote(
                zs.at[:, cols(c, wc)], zr.at[kind, slot, :, cols(c, wc)],
                z_s.at[c], z_r.at[kind, slot, c], tensor=inward,
            )

        def from_outside(c):
            return remote(
                zs.at[:, cols(c, wc)], zr.at[0, slot, :, cols(c, wc)],
                z_s.at[c], z_r.at[0, slot, c], tensor=inward,
            )

        def outward_copy(c):
            return remote(
                xm.at[:, cols(c, wc)], zr.at[1, slot, :, cols(c, wc)],
                t_s.at[c], z_r.at[1, slot, c], tensor=outward,
            )

        def relay(step, _):
            @pl.when(step < CHUNKS)
            def _():
                zs[:, cols(step, wc)] = jnp.dot(
                    mix[slot], wo_v[:, cols(step, wc)], preferred_element_type=jnp.float32
                ).astype(jnp.bfloat16)

                @pl.when(outer)
                def _():
                    inward_copy(step).start()

                @pl.when(jnp.logical_and(s == 0, m + 1 < M))
                def _():
                    take(m + 1, step)

            @pl.when(
                jnp.logical_and(
                    jnp.logical_not(outer),
                    jnp.logical_and(step >= EARLY, step < CHUNKS + EARLY),
                )
            )
            def _():
                c = step - EARLY
                from_outside(c).wait_recv()
                zs[:, cols(c, wc)] = (
                    zs[:, cols(c, wc)].astype(jnp.float32)
                    + zr[0, slot, :, cols(c, wc)].astype(jnp.float32)
                ).astype(jnp.bfloat16)
                inward_copy(c).start()

            @pl.when(jnp.logical_and(step == CHUNKS, m + 1 < M))
            def _():
                scale(m + 1)

            @pl.when(
                jnp.logical_and(
                    m + 1 < M,
                    jnp.logical_and(step >= CHUNKS, step < CHUNKS + QCHUNKS),
                )
            )
            def _():
                project(m + 1, step - CHUNKS)

            @pl.when(step >= EARLY + LAG)
            def _():
                c = step - EARLY - LAG
                outward_copy(c).wait_recv()

                @pl.when(middle)
                def _():
                    xm[:, cols(c, wc)] = (
                        xm[:, cols(c, wc)].astype(jnp.float32)
                        + (
                            zs[:, cols(c, wc)].astype(jnp.float32)
                            + zr[1, slot, :, cols(c, wc)].astype(jnp.float32)
                        )
                    ).astype(jnp.bfloat16)

                @pl.when(jnp.logical_not(middle))
                def _():
                    xm[:, cols(c, wc)] = zr[1, slot, :, cols(c, wc)]

                @pl.when(jnp.logical_not(outer))
                def _():
                    outward_copy(c).start()

                @pl.when(s == 0)
                def _():
                    handed(m, c).start()

                @pl.when(jnp.logical_and(s == 1, m < M // 2))
                def _():
                    finished_away(c).start()

                @pl.when(jnp.logical_and(s == 1, m >= M // 2))
                def _():
                    finished_here(c).start()

            return 0

        lax.fori_loop(0, CHUNKS + EARLY + LAG, relay, 0)

        def sent(c, _):
            inward_copy(c).wait_send()

            @pl.when(jnp.logical_not(outer))
            def _():
                outward_copy(c).wait_send()

            @pl.when(s == 0)
            def _():
                handed(m, c).wait_send()

            @pl.when(jnp.logical_and(s == 1, m < M // 2))
            def _():
                finished_away(c).wait_send()

            @pl.when(jnp.logical_and(s == 1, m >= M // 2))
            def _():
                finished_here(c).wait()

            return 0

        lax.fori_loop(0, CHUNKS, sent, 0)
        for r in range(D - 1):
            for h in range(kv_heads):
                mix_copy(r, h).wait_send()
        return carry

    lax.fori_loop(0, M, micro, 0)

    @pl.when(s == 0)
    def _():
        for r in range(D - 1):
            entry(r).wait_send()

        def returned(i, _):
            m, c = i // CHUNKS, lax.rem(i, CHUNKS)
            remote(
                xb.at[0, :, cols(c, wc)], out.at[rows(m * R, R), cols(c, wc)],
                h_s.at[c], h_r.at[m, c], section=1 - s,
            ).wait_recv()
            return 0

        lax.fori_loop(0, (M // 2) * CHUNKS, returned, 0)


def on_device(D, T, tokens, order, segments, gain, w_query, key_value_weight, w_out):
    R = D * BLOCK
    W = gain.shape[1]
    qcols = w_query.shape[2]
    wkv = key_value_weight[0].reshape(W, -1)
    qw = qcols + wkv.shape[1]
    kv_heads = key_value_weight.shape[2]
    bf16, f32 = jnp.bfloat16, jnp.float32
    vmem, hbm = pl.BlockSpec(memory_space=pltpu.VMEM), pl.BlockSpec(memory_space=pl.ANY)
    dma = pltpu.SemaphoreType.DMA
    return pl.pallas_call(
        functools.partial(kernel, D, T),
        out_shape=jax.ShapeDtypeStruct((M // 2 * R, W), bf16),
        in_specs=[hbm, vmem, vmem, vmem, hbm, hbm, hbm],
        out_specs=hbm,
        scratch_shapes=[
            pltpu.VMEM((W, qw), bf16),
            pltpu.VMEM((qcols, W), bf16),
            pltpu.VMEM((M * R, W), bf16),
            pltpu.VMEM((R, M * R), bf16),
            pltpu.VMEM((2, R, W), bf16),
            pltpu.VMEM((R, W), bf16),
            pltpu.VMEM((R, qw), bf16),
            pltpu.VMEM((2, D - 1, BLOCK, qw), bf16),
            pltpu.VMEM((R, 128), f32),
            pltpu.VMEM((2, D - 1, BLOCK, 128), f32),
            pltpu.VMEM((2, R, qcols), bf16),
            pltpu.VMEM((R, W), bf16),
            pltpu.VMEM((2, 2, R, W), bf16),
            dma((QCHUNKS,)),
            dma((CHUNKS,)),
            dma,
            dma((D - 1,)),
            dma((D - 1,)),
            dma((D - 1, QCHUNKS)),
            dma((2, D - 1, QCHUNKS)),
            dma((D - 1,)),
            dma((2, D - 1)),
            dma((D - 1, kv_heads)),
            dma((2, D - 1, kv_heads)),
            dma((CHUNKS,)),
            dma((2, 2, CHUNKS)),
            dma((CHUNKS,)),
            dma((CHUNKS,)),
            dma((M, CHUNKS)),
            dma((CHUNKS,)),
        ],
        compiler_params=pltpu.CompilerParams(
            collective_id=0, has_side_effects=True, vmem_limit_bytes=62 * 1024 * 1024
        ),
    )(
        tokens,
        order,
        segments,
        gain,
        w_query[0],
        wkv,
        w_out[0],
    )


def solution(mesh):
    placed = (
        P("dp", None),
        P(),
        P(),
        P("section", "dp"),
        P("section", "dp", "tensor"),
        P("section", "dp", "tensor", None),
        P("section", "tensor", "dp"),
    )
    return jax.shard_map(
        functools.partial(on_device, mesh.shape["dp"], mesh.shape["tensor"]),
        mesh=mesh, in_specs=placed, out_specs=P("section", "dp"), check_vma=False,
    )
```

```python
import functools
import math

import jax
import jax.numpy as jnp
from jax import lax
from jax.experimental import pallas as pl
from jax.experimental.pallas import tpu as pltpu
from jax.sharding import PartitionSpec as P

KEYVALUE_HEADS = 8
QUERY_HEADS = 64
HEAD = 128
SENTENCE_BLOCK = 32
BLOCK = 64
M = 2
QCHUNKS = 5
CHUNKS = 8
EARLY = 3
LAG = 2

norm_epsilon = 1e-05
MESH = pl.DeviceIdType.MESH


def kernel(
    D, T,
    tokens, order, segments, gain, wq, wkv, wo,
    out,
    wqkv_v, wo_v, ent, pick, xb, sc, qp, qr, sqp, sqr, mix, zs, zr,
    w_sem, wo_sem, own_sem, a_s, a_r, q_s, q_r, n_s, n_r, m_s, m_r,
    z_s, z_r, t_s, h_s, h_r, l_s,
):
    d = lax.axis_index("dp")
    s = lax.axis_index("section")
    t = lax.axis_index("tensor")
    R = D * BLOCK
    W = xb.shape[2]
    rows_in = tokens.shape[0]
    wc = W // CHUNKS
    qw = qp.shape[1]
    qc = qw // QCHUNKS
    half = T // 2
    is_left = t < half
    inward = jnp.where(is_left, t + 1, t - 1)
    outward = jnp.where(is_left, t - 1, t + 1)
    outer = jnp.logical_or(t == 0, t == T - 1)
    middle = jnp.logical_or(t == half - 1, t == half)
    kind = jnp.where(middle, 1, 0)
    assert BLOCK == 2 * SENTENCE_BLOCK
    kv_heads = KEYVALUE_HEADS // T
    group = QUERY_HEADS // KEYVALUE_HEADS
    qcols = kv_heads * group * HEAD
    peers = [lax.rem(d + r, D) for r in range(1, D)]

    def remote(src, dst, ss, rs, **where):
        return pltpu.make_async_remote_copy(
            src_ref=src, dst_ref=dst, send_sem=ss, recv_sem=rs,
            device_id=where, device_id_type=MESH,
        )

    def cols(c, width):
        return pl.ds(pl.multiple_of(c * width, width), width)

    def rows(start, count):
        return pl.ds(pl.multiple_of(start, BLOCK), count)

    def w_copy(j):
        if j < QCHUNKS - 1:
            return pltpu.make_async_copy(
                wq.at[:, pl.ds(j * qc, qc)], wqkv_v.at[:, pl.ds(j * qc, qc)], w_sem.at[j]
            )
        return pltpu.make_async_copy(wkv, wqkv_v.at[:, pl.ds(j * qc, qc)], w_sem.at[j])

    def wo_copy(c):
        return pltpu.make_async_copy(
            wo.at[:, cols(c, wc)], wo_v.at[:, cols(c, wc)], wo_sem.at[c]
        )

    own_tokens = pltpu.make_async_copy(
        tokens.at[:, cols(d, W)], ent.at[rows(d * rows_in, rows_in)], own_sem
    )

    def entry(r):
        peer = peers[r]
        return remote(
            tokens.at[:, cols(peer, W)], ent.at[rows(d * rows_in, rows_in)],
            a_s.at[r], a_r.at[r], dp=peer,
        )

    barrier = pltpu.get_barrier_semaphore()
    for peer in peers:
        pl.semaphore_signal(barrier, inc=1, device_id={"dp": peer}, device_id_type=MESH)
    pl.semaphore_signal(barrier, inc=1, device_id={"section": 1 - s}, device_id_type=MESH)

    @pl.when(t > 0)
    def _():
        pl.semaphore_signal(barrier, inc=1, device_id={"tensor": t - 1}, device_id_type=MESH)

    @pl.when(t < T - 1)
    def _():
        pl.semaphore_signal(barrier, inc=1, device_id={"tensor": t + 1}, device_id_type=MESH)

    pl.semaphore_wait(barrier, D + jnp.where(t > 0, 1, 0) + jnp.where(t < T - 1, 1, 0))

    @pl.when(s == 0)
    def _():
        for r in range(D - 1):
            entry(r).start()
        own_tokens.start()

    for j in range(QCHUNKS):
        w_copy(j).start()
    for c in range(CHUNKS):
        wo_copy(c).start()

    @pl.when(s == 0)
    def _():
        own_tokens.wait()
        for r in range(D - 1):
            entry(r).wait_recv()

    def handed(n, c):
        return remote(
            xb.at[lax.rem(n, 2), :, cols(c, wc)], ent.at[rows(n * R, R), cols(c, wc)],
            h_s.at[c], h_r.at[n, c], section=1 - s,
        )

    def norm_copy(n, r):
        return remote(
            sqp.at[rows(peers[r] * BLOCK, BLOCK)], sqr.at[lax.rem(n, 2), r],
            n_s.at[r], n_r.at[lax.rem(n, 2), r], dp=peers[r],
        )

    def q_copy(n, r, j):
        return remote(
            qp.at[rows(peers[r] * BLOCK, BLOCK), cols(j, qc)],
            qr.at[lax.rem(n, 2), r, :, cols(j, qc)],
            q_s.at[r, j], q_r.at[lax.rem(n, 2), r, j], dp=peers[r],
        )

    def choose(n):
        line = order[pl.ds(pl.multiple_of(n * R, R), R)].astype(jnp.float32)[None, :]
        down = lax.broadcasted_iota(jnp.int32, (R, R), 0)
        across = lax.broadcasted_iota(jnp.int32, (R, R), 1)
        column = jnp.sum(jnp.where(down == across, line, 0.0), axis=1, keepdims=True)
        places = lax.broadcasted_iota(jnp.int32, (R, M * R), 1).astype(jnp.float32)
        pick[...] = jnp.where(column == places, 1.0, 0.0).astype(jnp.bfloat16)

    def take(n, c):
        xb[lax.rem(n, 2), :, cols(c, wc)] = jnp.dot(
            pick[...], ent[:, cols(c, wc)], preferred_element_type=jnp.float32
        ).astype(jnp.bfloat16)

    def scale(n):
        @pl.when(s == 1)
        def _():
            def received(c, _):
                handed(n, c).wait_recv()
                xb[lax.rem(n, 2), :, cols(c, wc)] = ent[rows(n * R, R), cols(c, wc)]
                return 0

            lax.fori_loop(0, CHUNKS, received, 0)

        def one(c, total):
            wide = xb[lax.rem(n, 2), :, cols(c, wc)].astype(jnp.float32)
            sc[:, cols(c, wc)] = (wide * gain[:, cols(c, wc)]).astype(jnp.bfloat16)
            square = wide * wide
            for k in range(wc // 128):
                total = total + square[:, k * 128 : (k + 1) * 128]
            return total

        sqp[...] = lax.fori_loop(0, CHUNKS, one, jnp.zeros((R, 128), jnp.float32))
        for r in range(D - 1):
            norm_copy(n, r).start()

    def project(n, j):
        qp[:, cols(j, qc)] = jnp.dot(
            sc[...], wqkv_v[:, cols(j, qc)], preferred_element_type=jnp.float32
        ).astype(jnp.bfloat16)
        for r in range(D - 1):
            q_copy(n, r, j).start()

    @pl.when(s == 0)
    def _():
        choose(0)

        def first_take(c, _):
            take(0, c)
            return 0

        lax.fori_loop(0, CHUNKS, first_take, 0)

    scale(0)
    for j in range(QCHUNKS):
        w_copy(j).wait()

    def first_project(j, _):
        project(0, j)
        return 0

    lax.fori_loop(0, QCHUNKS, first_project, 0)

    own = rows(d * BLOCK, BLOCK)

    def micro(m, carry):
        slot = lax.rem(m, 2)
        mrow = m * R
        xm = xb.at[slot]

        def finished_away(c):
            return remote(
                xm.at[:, cols(c, wc)], out.at[rows(mrow, R), cols(c, wc)],
                h_s.at[c], h_r.at[m, c], section=1 - s,
            )

        def finished_here(c):
            return pltpu.make_async_copy(
                xm.at[:, cols(c, wc)],
                out.at[rows((m - M // 2) * R, R), cols(c, wc)],
                l_s.at[c],
            )

        line = segments[pl.ds(pl.multiple_of(mrow, R), R)].astype(jnp.float32)[None, :]
        down = lax.broadcasted_iota(jnp.int32, (BLOCK, R), 0) + d * BLOCK
        mine = down == lax.broadcasted_iota(jnp.int32, (BLOCK, R), 1)
        column = jnp.sum(jnp.where(mine, line, 0.0), axis=1, keepdims=True)
        same = jnp.where(column == line, 1.0, 0.0).astype(jnp.bfloat16)
        same = lax.dot_general(
            same, jnp.where(mine, 1.0, 0.0).astype(jnp.bfloat16),
            (((1,), (1,)), ((), ())), preferred_element_type=jnp.float32,
        )
        there = lax.broadcasted_iota(jnp.int32, (BLOCK, BLOCK), 1)
        here = lax.broadcasted_iota(jnp.int32, (BLOCK, BLOCK), 0)
        edge = jnp.where(here >= SENTENCE_BLOCK, SENTENCE_BLOCK, 0)
        allowed = jnp.where(jnp.logical_and(there <= here, there >= edge), same, 0.0)
        allowed = jnp.concatenate([allowed] * group, axis=0) > 0.5

        for r in range(D - 1):
            norm_copy(m, r).wait_recv()
        square = sqp[own, :]
        for r in range(D - 1):
            square = square + sqr[slot, r]
        rms = jnp.sqrt(
            jnp.sum(square, axis=1, keepdims=True) / (W * D) + norm_epsilon
        )

        def arrived(j, _):
            for r in range(D - 1):
                q_copy(m, r, j).wait_recv()
            return 0

        lax.fori_loop(0, QCHUNKS, arrived, 0)

        def summed(start, width):
            total = qp[own, pl.ds(start, width)].astype(jnp.float32)
            for r in range(D - 1):
                total = total + qr[slot, r, :, pl.ds(start, width)].astype(jnp.float32)
            return (total / rms).astype(jnp.bfloat16)

        def mix_copy(r, h):
            part = mix.at[own, pl.ds(h * group * HEAD, group * HEAD)]
            return remote(
                part, part, m_s.at[r, h], m_r.at[slot, r, h], dp=peers[r]
            )

        for h in range(kv_heads):
            lower = h * group * HEAD
            query = jnp.concatenate(
                [summed(lower + g * HEAD, HEAD) for g in range(group)], axis=0
            )
            key = summed(qcols + h * 2 * HEAD, HEAD)
            value = summed(qcols + h * 2 * HEAD + HEAD, HEAD)
            scores = lax.dot_general(
                query, key, (((1,), (1,)), ((), ())), preferred_element_type=jnp.float32
            ) / math.sqrt(HEAD)
            weights = jnp.where(allowed, jnp.exp(scores), 0.0)
            probs = (weights / jnp.sum(weights, axis=1, keepdims=True)).astype(jnp.bfloat16)
            mixed = jnp.dot(probs, value, preferred_element_type=jnp.float32).astype(
                jnp.bfloat16
            )
            for g in range(group):
                mix[own, pl.ds(lower + g * HEAD, HEAD)] = mixed[
                    g * BLOCK : (g + 1) * BLOCK
                ]
            for r in range(D - 1):
                mix_copy(r, h).start()

        def q_sent(j, _):
            for r in range(D - 1):
                q_copy(m, r, j).wait_send()
            return 0

        lax.fori_loop(0, QCHUNKS, q_sent, 0)
        for r in range(D - 1):
            norm_copy(m, r).wait_send()

        @pl.when(jnp.logical_and(s == 0, m + 1 < M))
        def _():
            choose(m + 1)

        @pl.when(m == 0)
        def _():
            for c in range(CHUNKS):
                wo_copy(c).wait()

        for h in range(kv_heads):
            for r in range(D - 1):
                mix_copy(r, h).wait_recv()

        def inward_copy(c):
            return remote(
                zs.at[:, cols(c, wc)], zr.at[kind * (1 + slot), :, cols(c, wc)],
                z_s.at[c], z_r.at[kind, slot, c], tensor=inward,
            )

        def from_outside(c):
            return remote(
                zs.at[:, cols(c, wc)], zr.at[0, :, cols(c, wc)],
                z_s.at[c], z_r.at[0, slot, c], tensor=inward,
            )

        def outward_copy(c):
            return remote(
                xm.at[:, cols(c, wc)], zr.at[1 + slot, :, cols(c, wc)],
                t_s.at[c], z_r.at[1, slot, c], tensor=outward,
            )

        def relay(step, _):
            @pl.when(step < CHUNKS)
            def _():
                zs[:, cols(step, wc)] = jnp.dot(
                    mix[...], wo_v[:, cols(step, wc)], preferred_element_type=jnp.float32
                ).astype(jnp.bfloat16)

                @pl.when(outer)
                def _():
                    inward_copy(step).start()

                @pl.when(jnp.logical_and(s == 0, m + 1 < M))
                def _():
                    take(m + 1, step)

            @pl.when(
                jnp.logical_and(
                    jnp.logical_not(outer),
                    jnp.logical_and(step >= EARLY, step < CHUNKS + EARLY),
                )
            )
            def _():
                c = step - EARLY
                from_outside(c).wait_recv()
                zs[:, cols(c, wc)] = (
                    zs[:, cols(c, wc)].astype(jnp.float32)
                    + zr[0, :, cols(c, wc)].astype(jnp.float32)
                ).astype(jnp.bfloat16)
                inward_copy(c).start()

            @pl.when(jnp.logical_and(step == CHUNKS, m + 1 < M))
            def _():
                scale(m + 1)

            @pl.when(
                jnp.logical_and(
                    m + 1 < M,
                    jnp.logical_and(step >= CHUNKS, step < CHUNKS + QCHUNKS),
                )
            )
            def _():
                project(m + 1, step - CHUNKS)

            @pl.when(step >= EARLY + LAG)
            def _():
                c = step - EARLY - LAG
                outward_copy(c).wait_recv()

                @pl.when(middle)
                def _():
                    xm[:, cols(c, wc)] = (
                        xm[:, cols(c, wc)].astype(jnp.float32)
                        + (
                            zs[:, cols(c, wc)].astype(jnp.float32)
                            + zr[1 + slot, :, cols(c, wc)].astype(jnp.float32)
                        )
                    ).astype(jnp.bfloat16)

                @pl.when(jnp.logical_not(middle))
                def _():
                    xm[:, cols(c, wc)] = zr[1 + slot, :, cols(c, wc)]

                @pl.when(jnp.logical_not(outer))
                def _():
                    outward_copy(c).start()

                @pl.when(s == 0)
                def _():
                    handed(m, c).start()

                @pl.when(jnp.logical_and(s == 1, m < M // 2))
                def _():
                    finished_away(c).start()

                @pl.when(jnp.logical_and(s == 1, m >= M // 2))
                def _():
                    finished_here(c).start()

            return 0

        lax.fori_loop(0, CHUNKS + EARLY + LAG, relay, 0)

        def sent(c, _):
            inward_copy(c).wait_send()

            @pl.when(jnp.logical_not(outer))
            def _():
                outward_copy(c).wait_send()

            @pl.when(s == 0)
            def _():
                handed(m, c).wait_send()

            @pl.when(jnp.logical_and(s == 1, m < M // 2))
            def _():
                finished_away(c).wait_send()

            @pl.when(jnp.logical_and(s == 1, m >= M // 2))
            def _():
                finished_here(c).wait()

            return 0

        lax.fori_loop(0, CHUNKS, sent, 0)
        for r in range(D - 1):
            for h in range(kv_heads):
                mix_copy(r, h).wait_send()
        return carry

    lax.fori_loop(0, M, micro, 0)

    @pl.when(s == 0)
    def _():
        for r in range(D - 1):
            entry(r).wait_send()

        def returned(i, _):
            m, c = i // CHUNKS, lax.rem(i, CHUNKS)
            remote(
                xb.at[0, :, cols(c, wc)], out.at[rows(m * R, R), cols(c, wc)],
                h_s.at[c], h_r.at[m, c], section=1 - s,
            ).wait_recv()
            return 0

        lax.fori_loop(0, (M // 2) * CHUNKS, returned, 0)


def on_device(D, T, tokens, order, segments, gain, w_query, key_value_weight, w_out):
    R = D * BLOCK
    W = gain.shape[1]
    qcols = w_query.shape[2]
    wkv = key_value_weight[0].reshape(W, -1)
    qw = qcols + wkv.shape[1]
    kv_heads = key_value_weight.shape[2]
    bf16, f32 = jnp.bfloat16, jnp.float32
    vmem, hbm = pl.BlockSpec(memory_space=pltpu.VMEM), pl.BlockSpec(memory_space=pl.ANY)
    dma = pltpu.SemaphoreType.DMA
    return pl.pallas_call(
        functools.partial(kernel, D, T),
        out_shape=jax.ShapeDtypeStruct((M // 2 * R, W), bf16),
        in_specs=[hbm, vmem, vmem, vmem, hbm, hbm, hbm],
        out_specs=hbm,
        scratch_shapes=[
            pltpu.VMEM((W, qw), bf16),
            pltpu.VMEM((qcols, W), bf16),
            pltpu.VMEM((M * R, W), bf16),
            pltpu.VMEM((R, M * R), bf16),
            pltpu.VMEM((2, R, W), bf16),
            pltpu.VMEM((R, W), bf16),
            pltpu.VMEM((R, qw), bf16),
            pltpu.VMEM((2, D - 1, BLOCK, qw), bf16),
            pltpu.VMEM((R, 128), f32),
            pltpu.VMEM((2, D - 1, BLOCK, 128), f32),
            pltpu.VMEM((R, qcols), bf16),
            pltpu.VMEM((R, W), bf16),
            pltpu.VMEM((3, R, W), bf16),
            dma((QCHUNKS,)),
            dma((CHUNKS,)),
            dma,
            dma((D - 1,)),
            dma((D - 1,)),
            dma((D - 1, QCHUNKS)),
            dma((2, D - 1, QCHUNKS)),
            dma((D - 1,)),
            dma((2, D - 1)),
            dma((D - 1, kv_heads)),
            dma((2, D - 1, kv_heads)),
            dma((CHUNKS,)),
            dma((2, 2, CHUNKS)),
            dma((CHUNKS,)),
            dma((CHUNKS,)),
            dma((M, CHUNKS)),
            dma((CHUNKS,)),
        ],
        compiler_params=pltpu.CompilerParams(
            collective_id=0, has_side_effects=True, vmem_limit_bytes=62 * 1024 * 1024
        ),
    )(
        tokens,
        order,
        segments,
        gain,
        w_query[0],
        wkv,
        w_out[0],
    )


def solution(mesh):
    placed = (
        P("dp", None),
        P(),
        P(),
        P("section", "dp"),
        P("section", "dp", "tensor"),
        P("section", "dp", "tensor", None),
        P("section", "tensor", "dp"),
    )
    return jax.shard_map(
        functools.partial(on_device, mesh.shape["dp"], mesh.shape["tensor"]),
        mesh=mesh, in_specs=placed, out_specs=P("section", "dp"), check_vma=False,
    )
```

```python
import functools
import math

import jax
import jax.numpy as jnp
from jax import lax
from jax.experimental import pallas as pl
from jax.experimental.pallas import tpu as pltpu
from jax.sharding import PartitionSpec as P

KEYVALUE_HEADS = 8
QUERY_HEADS = 64
HEAD = 128
SENTENCE_BLOCK = 32
BLOCK = 64
M = 2
QCHUNKS = 5
CHUNKS = 8
EARLY = 3
LAG = 2

norm_epsilon = 1e-05
MESH = pl.DeviceIdType.MESH


def kernel(
    D, T,
    tokens, order, segments, gain, wq, wkv, wo,
    out,
    wqkv_v, wo_v, ent, pick, xb, sc, qp, qr, sqp, sqr, mix, zs, zr,
    w_sem, wo_sem, own_sem, a_s, a_r, q_s, q_r, n_s, n_r, m_s, m_r,
    z_s, z_r, t_s, h_s, h_r, l_s,
):
    d = lax.axis_index("dp")
    s = lax.axis_index("section")
    t = lax.axis_index("tensor")
    R = D * BLOCK
    W = xb.shape[2]
    rows_in = tokens.shape[0]
    wc = W // CHUNKS
    qw = qp.shape[1]
    qc = qw // QCHUNKS
    half = T // 2
    is_left = t < half
    inward = jnp.where(is_left, t + 1, t - 1)
    outward = jnp.where(is_left, t - 1, t + 1)
    outer = jnp.logical_or(t == 0, t == T - 1)
    middle = jnp.logical_or(t == half - 1, t == half)
    kind = jnp.where(middle, 1, 0)
    assert BLOCK == 2 * SENTENCE_BLOCK
    kv_heads = KEYVALUE_HEADS // T
    group = QUERY_HEADS // KEYVALUE_HEADS
    qcols = kv_heads * group * HEAD
    peers = [lax.rem(d + r, D) for r in range(1, D)]

    def remote(src, dst, ss, rs, **where):
        return pltpu.make_async_remote_copy(
            src_ref=src, dst_ref=dst, send_sem=ss, recv_sem=rs,
            device_id=where, device_id_type=MESH,
        )

    def cols(c, width):
        return pl.ds(pl.multiple_of(c * width, width), width)

    def rows(start, count):
        return pl.ds(pl.multiple_of(start, BLOCK), count)

    def w_copy(j):
        if j < QCHUNKS - 1:
            return pltpu.make_async_copy(
                wq.at[:, pl.ds(j * qc, qc)], wqkv_v.at[:, pl.ds(j * qc, qc)], w_sem.at[j]
            )
        return pltpu.make_async_copy(wkv, wqkv_v.at[:, pl.ds(j * qc, qc)], w_sem.at[j])

    def wo_copy(c):
        return pltpu.make_async_copy(
            wo.at[:, cols(c, wc)], wo_v.at[:, cols(c, wc)], wo_sem.at[c]
        )

    own_tokens = pltpu.make_async_copy(
        tokens.at[:, cols(d, W)], ent.at[rows(d * rows_in, rows_in)], own_sem
    )

    def entry(r, c):
        peer = peers[r]
        return remote(
            tokens.at[:, cols(peer * CHUNKS + c, wc)],
            ent.at[rows(d * rows_in, rows_in), cols(c, wc)],
            a_s.at[r, c], a_r.at[r, c], dp=peer,
        )

    barrier = pltpu.get_barrier_semaphore()
    for peer in peers:
        pl.semaphore_signal(barrier, inc=1, device_id={"dp": peer}, device_id_type=MESH)
    pl.semaphore_signal(barrier, inc=1, device_id={"section": 1 - s}, device_id_type=MESH)

    @pl.when(t > 0)
    def _():
        pl.semaphore_signal(barrier, inc=1, device_id={"tensor": t - 1}, device_id_type=MESH)

    @pl.when(t < T - 1)
    def _():
        pl.semaphore_signal(barrier, inc=1, device_id={"tensor": t + 1}, device_id_type=MESH)

    pl.semaphore_wait(barrier, D + jnp.where(t > 0, 1, 0) + jnp.where(t < T - 1, 1, 0))

    @pl.when(s == 0)
    def _():
        own_tokens.start()

        def send(c, _):
            for r in range(D - 1):
                entry(r, c).start()
            return 0

        lax.fori_loop(0, CHUNKS, send, 0)

    for j in range(QCHUNKS):
        w_copy(j).start()
    for c in range(CHUNKS):
        wo_copy(c).start()

    def handed(n, c):
        return remote(
            xb.at[lax.rem(n, 2), :, cols(c, wc)], ent.at[rows(n * R, R), cols(c, wc)],
            h_s.at[c], h_r.at[n, c], section=1 - s,
        )

    def norm_copy(n, r):
        return remote(
            sqp.at[rows(peers[r] * BLOCK, BLOCK)], sqr.at[lax.rem(n, 2), r],
            n_s.at[r], n_r.at[lax.rem(n, 2), r], dp=peers[r],
        )

    def q_copy(n, r, j):
        return remote(
            qp.at[rows(peers[r] * BLOCK, BLOCK), cols(j, qc)],
            qr.at[lax.rem(n, 2), r, :, cols(j, qc)],
            q_s.at[r, j], q_r.at[lax.rem(n, 2), r, j], dp=peers[r],
        )

    def choose(n):
        line = order[pl.ds(pl.multiple_of(n * R, R), R)].astype(jnp.float32)[None, :]
        down = lax.broadcasted_iota(jnp.int32, (R, R), 0)
        across = lax.broadcasted_iota(jnp.int32, (R, R), 1)
        column = jnp.sum(jnp.where(down == across, line, 0.0), axis=1, keepdims=True)
        places = lax.broadcasted_iota(jnp.int32, (R, M * R), 1).astype(jnp.float32)
        pick[...] = jnp.where(column == places, 1.0, 0.0).astype(jnp.bfloat16)

    def take(n, c):
        xb[lax.rem(n, 2), :, cols(c, wc)] = jnp.dot(
            pick[...], ent[:, cols(c, wc)], preferred_element_type=jnp.float32
        ).astype(jnp.bfloat16)

    def scale(n, first=False):
        def one(c, total):
            @pl.when(s == 1)
            def _():
                handed(n, c).wait_recv()
                xb[lax.rem(n, 2), :, cols(c, wc)] = ent[rows(n * R, R), cols(c, wc)]

            if first:

                @pl.when(s == 0)
                def _():
                    for r in range(D - 1):
                        entry(r, c).wait_recv()
                    take(n, c)

            wide = xb[lax.rem(n, 2), :, cols(c, wc)].astype(jnp.float32)
            sc[:, cols(c, wc)] = (wide * gain[:, cols(c, wc)]).astype(jnp.bfloat16)
            square = wide * wide
            for k in range(wc // 128):
                total = total + square[:, k * 128 : (k + 1) * 128]
            return total

        sqp[...] = lax.fori_loop(0, CHUNKS, one, jnp.zeros((R, 128), jnp.float32))
        for r in range(D - 1):
            norm_copy(n, r).start()

    def project(n, j):
        qp[:, cols(j, qc)] = jnp.dot(
            sc[...], wqkv_v[:, cols(j, qc)], preferred_element_type=jnp.float32
        ).astype(jnp.bfloat16)
        for r in range(D - 1):
            q_copy(n, r, j).start()

    @pl.when(s == 0)
    def _():
        choose(0)
        own_tokens.wait()

    scale(0, True)
    for j in range(QCHUNKS):
        w_copy(j).wait()

    def first_project(j, _):
        project(0, j)
        return 0

    lax.fori_loop(0, QCHUNKS, first_project, 0)

    own = rows(d * BLOCK, BLOCK)

    def micro(m, carry):
        slot = lax.rem(m, 2)
        mrow = m * R
        xm = xb.at[slot]

        def finished_away(c):
            return remote(
                xm.at[:, cols(c, wc)], out.at[rows(mrow, R), cols(c, wc)],
                h_s.at[c], h_r.at[m, c], section=1 - s,
            )

        def finished_here(c):
            return pltpu.make_async_copy(
                xm.at[:, cols(c, wc)],
                out.at[rows((m - M // 2) * R, R), cols(c, wc)],
                l_s.at[c],
            )

        line = segments[pl.ds(pl.multiple_of(mrow, R), R)].astype(jnp.float32)[None, :]
        down = lax.broadcasted_iota(jnp.int32, (BLOCK, R), 0) + d * BLOCK
        mine = down == lax.broadcasted_iota(jnp.int32, (BLOCK, R), 1)
        column = jnp.sum(jnp.where(mine, line, 0.0), axis=1, keepdims=True)
        same = jnp.where(column == line, 1.0, 0.0).astype(jnp.bfloat16)
        same = lax.dot_general(
            same, jnp.where(mine, 1.0, 0.0).astype(jnp.bfloat16),
            (((1,), (1,)), ((), ())), preferred_element_type=jnp.float32,
        )
        there = lax.broadcasted_iota(jnp.int32, (BLOCK, BLOCK), 1)
        here = lax.broadcasted_iota(jnp.int32, (BLOCK, BLOCK), 0)
        edge = jnp.where(here >= SENTENCE_BLOCK, SENTENCE_BLOCK, 0)
        allowed = jnp.where(jnp.logical_and(there <= here, there >= edge), same, 0.0)
        allowed = jnp.concatenate([allowed] * group, axis=0) > 0.5

        for r in range(D - 1):
            norm_copy(m, r).wait_recv()
        square = sqp[own, :]
        for r in range(D - 1):
            square = square + sqr[slot, r]
        rms = jnp.sqrt(
            jnp.sum(square, axis=1, keepdims=True) / (W * D) + norm_epsilon
        )

        def arrived(j, _):
            for r in range(D - 1):
                q_copy(m, r, j).wait_recv()
            return 0

        lax.fori_loop(0, QCHUNKS, arrived, 0)

        def summed(start, width):
            total = qp[own, pl.ds(start, width)].astype(jnp.float32)
            for r in range(D - 1):
                total = total + qr[slot, r, :, pl.ds(start, width)].astype(jnp.float32)
            return (total / rms).astype(jnp.bfloat16)

        def mix_copy(r, h):
            part = mix.at[own, pl.ds(h * group * HEAD, group * HEAD)]
            return remote(
                part, part, m_s.at[r, h], m_r.at[slot, r, h], dp=peers[r]
            )

        for h in range(kv_heads):
            lower = h * group * HEAD
            query = jnp.concatenate(
                [summed(lower + g * HEAD, HEAD) for g in range(group)], axis=0
            )
            key = summed(qcols + h * 2 * HEAD, HEAD)
            value = summed(qcols + h * 2 * HEAD + HEAD, HEAD)
            scores = lax.dot_general(
                query, key, (((1,), (1,)), ((), ())), preferred_element_type=jnp.float32
            ) / math.sqrt(HEAD)
            weights = jnp.where(allowed, jnp.exp(scores), 0.0)
            probs = (weights / jnp.sum(weights, axis=1, keepdims=True)).astype(jnp.bfloat16)
            mixed = jnp.dot(probs, value, preferred_element_type=jnp.float32).astype(
                jnp.bfloat16
            )
            for g in range(group):
                mix[own, pl.ds(lower + g * HEAD, HEAD)] = mixed[
                    g * BLOCK : (g + 1) * BLOCK
                ]
            for r in range(D - 1):
                mix_copy(r, h).start()

        def q_sent(j, _):
            for r in range(D - 1):
                q_copy(m, r, j).wait_send()
            return 0

        lax.fori_loop(0, QCHUNKS, q_sent, 0)
        for r in range(D - 1):
            norm_copy(m, r).wait_send()

        @pl.when(jnp.logical_and(s == 0, m + 1 < M))
        def _():
            choose(m + 1)

        @pl.when(m == 0)
        def _():
            for c in range(CHUNKS):
                wo_copy(c).wait()

        for h in range(kv_heads):
            for r in range(D - 1):
                mix_copy(r, h).wait_recv()

        def inward_copy(c):
            return remote(
                zs.at[:, cols(c, wc)], zr.at[kind * (1 + slot), :, cols(c, wc)],
                z_s.at[c], z_r.at[kind, slot, c], tensor=inward,
            )

        def from_outside(c):
            return remote(
                zs.at[:, cols(c, wc)], zr.at[0, :, cols(c, wc)],
                z_s.at[c], z_r.at[0, slot, c], tensor=inward,
            )

        def outward_copy(c):
            return remote(
                xm.at[:, cols(c, wc)], zr.at[1 + slot, :, cols(c, wc)],
                t_s.at[c], z_r.at[1, slot, c], tensor=outward,
            )

        def relay(step, _):
            @pl.when(step < CHUNKS)
            def _():
                zs[:, cols(step, wc)] = jnp.dot(
                    mix[...], wo_v[:, cols(step, wc)], preferred_element_type=jnp.float32
                ).astype(jnp.bfloat16)

                @pl.when(outer)
                def _():
                    inward_copy(step).start()

                @pl.when(jnp.logical_and(s == 0, m + 1 < M))
                def _():
                    take(m + 1, step)

            @pl.when(
                jnp.logical_and(
                    jnp.logical_not(outer),
                    jnp.logical_and(step >= EARLY, step < CHUNKS + EARLY),
                )
            )
            def _():
                c = step - EARLY
                from_outside(c).wait_recv()
                zs[:, cols(c, wc)] = (
                    zs[:, cols(c, wc)].astype(jnp.float32)
                    + zr[0, :, cols(c, wc)].astype(jnp.float32)
                ).astype(jnp.bfloat16)
                inward_copy(c).start()

            @pl.when(jnp.logical_and(step == CHUNKS, m + 1 < M))
            def _():
                scale(m + 1)

            @pl.when(
                jnp.logical_and(
                    m + 1 < M,
                    jnp.logical_and(step >= CHUNKS, step < CHUNKS + QCHUNKS),
                )
            )
            def _():
                project(m + 1, step - CHUNKS)

            @pl.when(step >= EARLY + LAG)
            def _():
                c = step - EARLY - LAG
                outward_copy(c).wait_recv()

                @pl.when(middle)
                def _():
                    xm[:, cols(c, wc)] = (
                        xm[:, cols(c, wc)].astype(jnp.float32)
                        + (
                            zs[:, cols(c, wc)].astype(jnp.float32)
                            + zr[1 + slot, :, cols(c, wc)].astype(jnp.float32)
                        )
                    ).astype(jnp.bfloat16)

                @pl.when(jnp.logical_not(middle))
                def _():
                    xm[:, cols(c, wc)] = zr[1 + slot, :, cols(c, wc)]

                @pl.when(jnp.logical_not(outer))
                def _():
                    outward_copy(c).start()

                @pl.when(s == 0)
                def _():
                    handed(m, c).start()

                @pl.when(jnp.logical_and(s == 1, m < M // 2))
                def _():
                    finished_away(c).start()

                @pl.when(jnp.logical_and(s == 1, m >= M // 2))
                def _():
                    finished_here(c).start()

            return 0

        lax.fori_loop(0, CHUNKS + EARLY + LAG, relay, 0)

        def sent(c, _):
            inward_copy(c).wait_send()

            @pl.when(jnp.logical_not(outer))
            def _():
                outward_copy(c).wait_send()

            @pl.when(s == 0)
            def _():
                handed(m, c).wait_send()

            @pl.when(jnp.logical_and(s == 1, m < M // 2))
            def _():
                finished_away(c).wait_send()

            @pl.when(jnp.logical_and(s == 1, m >= M // 2))
            def _():
                finished_here(c).wait()

            return 0

        lax.fori_loop(0, CHUNKS, sent, 0)
        for r in range(D - 1):
            for h in range(kv_heads):
                mix_copy(r, h).wait_send()
        return carry

    lax.fori_loop(0, M, micro, 0)

    @pl.when(s == 0)
    def _():
        def entered(c, _):
            for r in range(D - 1):
                entry(r, c).wait_send()
            return 0

        lax.fori_loop(0, CHUNKS, entered, 0)

        def returned(i, _):
            m, c = i // CHUNKS, lax.rem(i, CHUNKS)
            remote(
                xb.at[0, :, cols(c, wc)], out.at[rows(m * R, R), cols(c, wc)],
                h_s.at[c], h_r.at[m, c], section=1 - s,
            ).wait_recv()
            return 0

        lax.fori_loop(0, (M // 2) * CHUNKS, returned, 0)


def on_device(D, T, tokens, order, segments, gain, w_query, key_value_weight, w_out):
    R = D * BLOCK
    W = gain.shape[1]
    qcols = w_query.shape[2]
    wkv = key_value_weight[0].reshape(W, -1)
    qw = qcols + wkv.shape[1]
    kv_heads = key_value_weight.shape[2]
    bf16, f32 = jnp.bfloat16, jnp.float32
    vmem, hbm = pl.BlockSpec(memory_space=pltpu.VMEM), pl.BlockSpec(memory_space=pl.ANY)
    dma = pltpu.SemaphoreType.DMA
    return pl.pallas_call(
        functools.partial(kernel, D, T),
        out_shape=jax.ShapeDtypeStruct((M // 2 * R, W), bf16),
        in_specs=[hbm, vmem, vmem, vmem, hbm, hbm, hbm],
        out_specs=hbm,
        scratch_shapes=[
            pltpu.VMEM((W, qw), bf16),
            pltpu.VMEM((qcols, W), bf16),
            pltpu.VMEM((M * R, W), bf16),
            pltpu.VMEM((R, M * R), bf16),
            pltpu.VMEM((2, R, W), bf16),
            pltpu.VMEM((R, W), bf16),
            pltpu.VMEM((R, qw), bf16),
            pltpu.VMEM((2, D - 1, BLOCK, qw), bf16),
            pltpu.VMEM((R, 128), f32),
            pltpu.VMEM((2, D - 1, BLOCK, 128), f32),
            pltpu.VMEM((R, qcols), bf16),
            pltpu.VMEM((R, W), bf16),
            pltpu.VMEM((3, R, W), bf16),
            dma((QCHUNKS,)),
            dma((CHUNKS,)),
            dma,
            dma((D - 1, CHUNKS)),
            dma((D - 1, CHUNKS)),
            dma((D - 1, QCHUNKS)),
            dma((2, D - 1, QCHUNKS)),
            dma((D - 1,)),
            dma((2, D - 1)),
            dma((D - 1, kv_heads)),
            dma((2, D - 1, kv_heads)),
            dma((CHUNKS,)),
            dma((2, 2, CHUNKS)),
            dma((CHUNKS,)),
            dma((CHUNKS,)),
            dma((M, CHUNKS)),
            dma((CHUNKS,)),
        ],
        compiler_params=pltpu.CompilerParams(
            collective_id=0, has_side_effects=True, vmem_limit_bytes=62 * 1024 * 1024
        ),
    )(
        tokens,
        order,
        segments,
        gain,
        w_query[0],
        wkv,
        w_out[0],
    )


def solution(mesh):
    placed = (
        P("dp", None),
        P(),
        P(),
        P("section", "dp"),
        P("section", "dp", "tensor"),
        P("section", "dp", "tensor", None),
        P("section", "tensor", "dp"),
    )
    return jax.shard_map(
        functools.partial(on_device, mesh.shape["dp"], mesh.shape["tensor"]),
        mesh=mesh, in_specs=placed, out_specs=P("section", "dp"), check_vma=False,
    )
```
